512 devices in a mesh: ctx: 32 (over z, x_lo, core), head: 16 (over x_hi, y).
Axes of the slice: x: 4 (x_hi: 2, x_lo: 2; x = x_hi * 2 + x_lo), y: 8, z: 8, core: 2. Of those that a mesh axis runs over, the one named last changes fastest.
Arguments:
- queries: bfloat16 [6144, 4096], P('ctx', 'head'), may hold values from -30 to 30
- keys: bfloat16 [6144, 1024], P('ctx'), may hold values from -6 to 6
- values: bfloat16 [6144, 1024], P('ctx'), may hold values from -6 to 6
- out_grad: bfloat16 [6144, 4096], P('ctx', 'head'), may hold values from -6 to 6
- positions: int32 [6144], P('ctx'), may hold values from 0 to 6143, as said below
Outputs:
- query_grad: bfloat16 [6144, 4096], P('ctx', 'head')
- key_fisher: float32 [16, 64], P('head')
- value_fisher: float32 [16, 64], P('head')
The draws below stay inside these ranges and needn't reach their ends.
Inputs may be any that keep to these rules, and one draw needn't show every extreme that they name: Each aligned block of 96 rows holds 96 consecutive positions in increasing order; the blocks' order is a permutation of all 64 blocks, so positions is a permutation of the document.
All inputs are finite; a program needn't handle non-finite values.
Results may differ from the reference program's by a relative error of at most 0.009.
The reference program's roundings to bfloat16 on the way (of `query_rot`, `key_rot`, `dscore` and `probs_low`) count: a program that leaves them out, or rounds other values in their place, can miss the bound.
Values may be sent and summed in bfloat16 or wider, within the bound.
No kernel may reach another device: no remote copies, remote signals or barrier semaphores. Data moves between devices by JAX's collectives and lax.ppermute only.
A program may use at most 128 MiB of HBM per device.

```python
import math
import jax
import jax.numpy as jnp
from jax import lax

HD = 128
GROUP = 4
HEADS = 32
KV_HEADS = 8
SEQ = 6144
BLOCK = 96


def shared_keys(key):
    return jnp.clip(jax.random.normal(key, (SEQ, KV_HEADS * HD), jnp.float32), -6.0, 6.0)


def draw_keys(key, part):
    base = shared_keys(key)
    return base.astype(jnp.bfloat16)


def draw_queries(key, part):
    key = jax.random.fold_in(key, 5)
    fresh = jnp.clip(3.0 * jax.random.normal(key, (SEQ, HEADS * HD), jnp.float32), -30.0, 30.0)
    return fresh.astype(jnp.bfloat16)


def draw_positions(key, part):
    key = jax.random.fold_in(key, 9)
    number = SEQ // BLOCK
    order = jax.random.permutation(key, number).astype(jnp.int32)
    within = jnp.arange(BLOCK, dtype=jnp.int32)
    return (order[:, None] * BLOCK + within[None, :]).reshape(SEQ).astype(jnp.int32)


def block_levels(rng, shape, shards, low, high):
    factor_of, own = 1.0, jax.random.fold_in(rng, 6)
    for position, parts in shards:
        steps = jnp.exp(jax.random.uniform(jax.random.fold_in(own, position), (parts,), jnp.float32, low / len(shards), high / len(shards)))
        factor_of = factor_of * jnp.repeat(steps, shape[position] // parts).reshape([-1 if axis == position else 1 for axis in range(len(shape))])
    return factor_of


def bell_draw(key, extent, spread, bound, shards=(), kind=jnp.bfloat16):
    array = spread * jax.random.normal(key, extent, jnp.float32)
    if shards:
        array = array * block_levels(key, extent, shards, -0.22, 0.18)
    return jnp.clip(array, -bound, bound).astype(kind)


def setup_inputs(seed: int = 0) -> dict:
    key_of = jax.random.split(jax.random.key(seed), 6)
    return {
        "queries": draw_queries(jax.random.fold_in(key_of[5], 71), 0),
        "keys": draw_keys(jax.random.fold_in(key_of[5], 71), 0),
        "values": bell_draw(key_of[2], (SEQ, KV_HEADS * HD), 1.0, 6.0, ((0, 32),)),
        "out_grad": bell_draw(key_of[3], (SEQ, HEADS * HD), 1.0, 6.0, ((0, 32), (1, 16))),
        "positions": draw_positions(jax.random.fold_in(key_of[5], 71), 0),
    }


NEGATIVE_FILL = -1.0e30


def angles_of(pos_table, width):
    half_width = width // 2
    frequency = 500000.0 ** (-(jnp.arange(half_width, dtype=jnp.float32) * 2.0 / width))
    wavelength = 2.0 * math.pi / frequency
    smooth = jnp.clip((8192.0 / wavelength - 1.0) / 3.0, 0.0, 1.0)
    frequency = (1.0 - smooth) * frequency / 8.0 + smooth * frequency
    return pos_table.astype(jnp.float32)[:, None, None] * frequency[None, None, :]


def rotate(vector, angle):
    half_width = vector.shape[-1] // 2
    leading = vector[..., :half_width]
    trailing = vector[..., half_width:]
    cosine = jnp.cos(angle)
    sin_part = jnp.sin(angle)
    return jnp.concatenate([leading * cosine - trailing * sin_part, trailing * cosine + leading * sin_part], axis=-1)


def unrotate(vector, angle):
    half_width = vector.shape[-1] // 2
    leading = vector[..., :half_width]
    trailing = vector[..., half_width:]
    cosine = jnp.cos(angle)
    sin_part = jnp.sin(angle)
    return jnp.concatenate([leading * cosine + trailing * sin_part, trailing * cosine - leading * sin_part], axis=-1)


def reference(queries, keys, values, out_grad, positions):
    scale = HD ** -0.5
    length = queries.shape[0]
    angle = angles_of(positions, HD)
    query_rot = rotate(queries.reshape(length, HEADS, HD).astype(jnp.float32), angle).astype(jnp.bfloat16)
    key_rot = rotate(keys.reshape(length, KV_HEADS, HD).astype(jnp.float32), angle).astype(jnp.bfloat16)
    value_heads = values.reshape(length, KV_HEADS, HD)
    grad_heads = out_grad.reshape(length, HEADS, HD)
    visible = positions[None, :] <= positions[:, None]

    def one_head(head_index):
        group_index = head_index // GROUP
        query = lax.dynamic_index_in_dim(query_rot, head_index, 1, keepdims=False)
        key_one = lax.dynamic_index_in_dim(key_rot, group_index, 1, keepdims=False)
        value_one = lax.dynamic_index_in_dim(value_heads, group_index, 1, keepdims=False)
        grad_one = lax.dynamic_index_in_dim(grad_heads, head_index, 1, keepdims=False)
        scores = jnp.dot(query, key_one.T, preferred_element_type=jnp.float32) * scale
        largest = jnp.max(jnp.where(visible, scores, NEGATIVE_FILL), axis=1)
        summed = jnp.sum(jnp.where(visible, jnp.exp(scores - largest[:, None]), 0.0), axis=1)
        lse = largest + jnp.log(summed)
        dprob = jnp.dot(grad_one, value_one.T, preferred_element_type=jnp.float32)
        probs = jnp.where(visible, jnp.exp(scores - lse[:, None]), 0.0)
        delta = jnp.sum(probs * dprob, axis=1)
        dscore = (probs * (dprob - delta[:, None])).astype(jnp.bfloat16)
        probs_low = probs.astype(jnp.bfloat16)
        dq_head = jnp.dot(dscore, key_one, preferred_element_type=jnp.float32)
        dk_head = jnp.dot(dscore.T, query, preferred_element_type=jnp.float32)
        dv_head = jnp.dot(probs_low.T, grad_one, preferred_element_type=jnp.float32)
        return dq_head, dk_head, dv_head

    dq_all, dk_all, dv_all = lax.map(one_head, jnp.arange(HEADS, dtype=jnp.int32))
    dq_rot = jnp.transpose(dq_all, (1, 0, 2)) * scale
    query_grad = unrotate(dq_rot, angle).reshape(length, HEADS * HD).astype(jnp.bfloat16)
    dk_rot = jnp.transpose(jnp.sum(dk_all.reshape(KV_HEADS, GROUP, length, HD), axis=1), (1, 0, 2)) * scale
    dv_sum = jnp.transpose(jnp.sum(dv_all.reshape(KV_HEADS, GROUP, length, HD), axis=1), (1, 0, 2))
    key_pre = unrotate(dk_rot, angle)
    key_fisher = jnp.mean(key_pre * key_pre, axis=0).reshape(KV_HEADS * 2, HD // 2)
    value_fisher = jnp.mean(dv_sum * dv_sum, axis=0).reshape(KV_HEADS * 2, HD // 2)
    return query_grad, key_fisher, value_fisher
```

```python
import functools
import math

import jax
import jax.numpy as jnp
import numpy as np
from jax import lax
from jax.experimental import pallas as pl
from jax.experimental.pallas import tpu as pltpu
from jax.sharding import Mesh
from jax.sharding import PartitionSpec as P

HD = 128
SEQ = 6144
BLOCK = 96
TOK = 192
PACK = TOK + 16
SCALE = HD ** (-0.5)
LOG2E = math.log2(math.e)
FILL = -1e30
FLOOR = -1e29
MIB = 1024 * 1024
VMEM = 20 * MIB
VMEM_LARGE = 40 * MIB
VMEM_ALL = 60 * MIB
ROWS = 2 * TOK + 16
AX_Z, AX_X, AX_C = "z", "xl", "core"
QGROUP = (AX_X, AX_C)
KGROUP = (AX_Z, "yl")
ALLGROUP = (AX_Z, AX_X, AX_C, "yl")
NQ = 4
NK = 8
NALL = 2 * NQ * NK
QL = 2 * NQ * TOK
STAT = QL // HD
QT = 384


def frequencies():
    half = HD // 2
    freq = np.float32(500000.0) ** (-(np.arange(half, dtype=np.float32) * np.float32(2.0) / np.float32(HD)))
    freq = freq.astype(np.float32)
    wave = (np.float32(2.0 * math.pi) / freq).astype(np.float32)
    smooth = np.clip((np.float32(8192.0) / wave - np.float32(1.0)) / np.float32(3.0), 0.0, 1.0).astype(np.float32)
    freq = (np.float32(1.0) - smooth) * freq / np.float32(8.0) + smooth * freq
    return np.concatenate([freq, freq]).astype(np.float32)[None, :]


def dot(a, b, ca, cb):
    return lax.dot_general(a, b, (((ca,), (cb,)), ((), ())), preferred_element_type=jnp.float32)


def smem():
    return pl.BlockSpec(memory_space=pltpu.SMEM)


def vmem():
    return pl.BlockSpec(memory_space=pltpu.VMEM)


def rotate(x, cosine, sine):
    x = x.astype(jnp.float32)
    return (x * cosine + pltpu.roll(x, HD // 2, 1) * sine).astype(jnp.bfloat16)


def id_rows(pos_ref, j):
    block = lax.div(pos_ref[j * BLOCK], BLOCK).astype(jnp.float32)
    return jnp.full((PACK - TOK, HD), block, jnp.float32).astype(jnp.bfloat16)


def key_kernel(kvi_ref, pos_ref, freq_ref, k_ref, v_ref, kv_ref, cs_ref):
    row = lax.broadcasted_iota(jnp.int32, (TOK, HD), 0)
    pos = jnp.where(row < BLOCK, pos_ref[0] + row, pos_ref[BLOCK] + row - BLOCK)
    angle = pos.astype(jnp.float32) * freq_ref[...]
    cosine = jnp.cos(angle)
    lane = lax.broadcasted_iota(jnp.int32, (TOK, HD), 1)
    sine = jnp.sin(angle)
    sine = jnp.where(lane < HD // 2, -sine, sine)
    cs_ref[0] = cosine
    cs_ref[1] = sine
    key = rotate(k_ref[...], cosine, sine)
    lanes = lax.broadcasted_iota(jnp.int32, (ROWS - 2 * TOK, HD), 1)
    first, second = (lax.div(pos_ref[j * BLOCK], BLOCK) for j in range(2))
    ids = jnp.where(lanes < HD // 2, first, second).astype(jnp.float32).astype(jnp.bfloat16)
    for i in range(NK):
        kv_ref[i, :TOK, :] = key
        kv_ref[i, TOK : 2 * TOK, :] = v_ref[...]
        kv_ref[i, 2 * TOK :, :] = ids


def prep_keys(kvi, positions, freq, keys, values):
    whole = lambda *shape: pl.BlockSpec(shape, lambda i, kvi, pos: (0,) * len(shape))
    picked = pl.BlockSpec((TOK, HD), lambda i, kvi, pos: (0, kvi[0]))
    return pl.pallas_call(
        key_kernel,
        grid_spec=pltpu.PrefetchScalarGridSpec(
            num_scalar_prefetch=2,
            grid=(1,),
            in_specs=[whole(1, HD), picked, picked],
            out_specs=[whole(NK, ROWS, HD), whole(2, TOK, HD)],
        ),
        out_shape=[
            jax.ShapeDtypeStruct((NK, ROWS, HD), jnp.bfloat16),
            jax.ShapeDtypeStruct((2, TOK, HD), jnp.float32),
        ],
        compiler_params=pltpu.CompilerParams(vmem_limit_bytes=VMEM_ALL),
        cost_estimate=pl.CostEstimate(flops=10**6, bytes_accessed=10**6, transcendentals=10**5),
        name="rotate_keys",
    )(kvi, positions, freq, keys, values)


def query_kernel(pos_ref, cs_ref, q_ref, g_ref, qg_ref):
    for head in range(2):
        cols = slice(head * HD, (head + 1) * HD)
        qg_ref[:TOK, cols] = rotate(q_ref[:, cols], cs_ref[0], cs_ref[1])
    qg_ref[:TOK, 2 * HD :] = g_ref[...]
    for j in range(4):
        qg_ref[TOK:, j * HD : (j + 1) * HD] = id_rows(pos_ref, j % 2)


def prep_queries(positions, cs, queries, out_grad):
    return pl.pallas_call(
        query_kernel,
        in_specs=[smem()] + [vmem()] * 3,
        out_specs=vmem(),
        out_shape=jax.ShapeDtypeStruct((PACK, 4 * HD), jnp.bfloat16),
        compiler_params=pltpu.CompilerParams(vmem_limit_bytes=VMEM),
        cost_estimate=pl.CostEstimate(flops=10**6, bytes_accessed=10**6, transcendentals=0),
        name="rotate_queries",
    )(positions, cs, queries, out_grad)


def block_id(ref, column):
    rows = ref[TOK:PACK, column * HD : (column + 1) * HD]
    return jnp.max(rows.astype(jnp.float32)).astype(jnp.int32)


def key_ids(kv_ref, c):
    rows = kv_ref[c, 2 * TOK :, :].astype(jnp.float32)
    lanes = lax.broadcasted_iota(jnp.int32, rows.shape, 1)
    masked = (jnp.where(lanes < HD // 2, rows, 0.0), jnp.where(lanes < HD // 2, 0.0, rows))
    return [jnp.max(x).astype(jnp.int32) for x in masked]


def ranks_of(ids):
    count = len(ids)
    return [sum((ids[i] < ids[j]).astype(jnp.int32) for i in range(count) if i != j) for j in range(count)]


def query_positions(perm_ref, first):
    lane = lax.broadcasted_iota(jnp.int32, (1, QL - first * QT), 1)
    pos = jnp.zeros(lane.shape, jnp.int32)
    for r in range(2 * first, 2 * NQ):
        for head in range(2):
            start = (r - 2 * first) * TOK + head * BLOCK
            pos = jnp.where(lane >= start, perm_ref[8 + r] * BLOCK - start + lane, pos)
    return pos


def key_positions(perm_ref, pair):
    row = lax.broadcasted_iota(jnp.int32, (TOK, 1), 0)
    low, high = perm_ref[32 + 2 * pair], perm_ref[33 + 2 * pair]
    return row + jnp.where(row < BLOCK, low * BLOCK, (high - 1) * BLOCK)


def first_tile(perm_ref, pair):
    low = perm_ref[32 + 2 * pair]
    return sum((perm_ref[9 + 2 * t] < low).astype(jnp.int32) for t in range(NQ))


def block_rows(start, count):
    return pl.ds(pl.multiple_of(start, BLOCK), count)


def stats_kernel(q0, q1, q2, q3, kv_ref, st_ref, qs_ref, gs_ref, ks_ref, vs_ref, perm_ref, m_ref, l_ref, a_ref):
    slots = (q0, q1, q2, q3)
    ids = [block_id(ref, j) for ref in slots for j in range(2)]
    for j, r in enumerate(ranks_of(ids)):
        perm_ref[r] = j
        perm_ref[8 + r] = ids[j]
        ref, rows = slots[j // 2], slice((j % 2) * BLOCK, (j % 2 + 1) * BLOCK)
        for head in range(2):
            to = block_rows(r * TOK + head * BLOCK, BLOCK)
            qs_ref[to, :] = ref[rows, head * HD : (head + 1) * HD]
            gs_ref[to, :] = ref[rows, (2 + head) * HD : (3 + head) * HD]
    ids = [x for c in range(NK) for x in key_ids(kv_ref, c)]
    for j, r in enumerate(ranks_of(ids)):
        perm_ref[16 + r] = j
        perm_ref[32 + r] = ids[j]
        rows = slice((j % 2) * BLOCK, (j % 2 + 1) * BLOCK)
        to = block_rows(r * BLOCK, BLOCK)
        ks_ref[to, :] = kv_ref[j // 2, rows, :]
        vs_ref[to, :] = kv_ref[j // 2, slice(TOK + rows.start, TOK + rows.stop), :]
    m_ref[...] = jnp.full(m_ref.shape, FLOOR, jnp.float32)
    l_ref[...] = jnp.zeros(l_ref.shape, jnp.float32)
    a_ref[...] = jnp.zeros(a_ref.shape, jnp.float32)

    def step(pair, _):
        rows = block_rows(pair * TOK, TOK)
        tile = first_tile(perm_ref, pair)
        for first in range(NQ):

            @pl.when(tile == first)
            def _():
                cols = slice(first * QT, QL)
                s = dot(ks_ref[rows, :], qs_ref[cols, :], 1, 1) * (SCALE * LOG2E)
                d = dot(vs_ref[rows, :], gs_ref[cols, :], 1, 1)
                visible = key_positions(perm_ref, pair) <= query_positions(perm_ref, first)
                s = jnp.where(visible, s, FILL)
                m = m_ref[:, cols]
                m2 = jnp.maximum(m, jnp.max(s, axis=0, keepdims=True))
                p = jnp.exp2(s - m2)
                alpha = jnp.exp2(m - m2)
                m_ref[:, cols] = m2
                l_ref[:, cols] = alpha * l_ref[:, cols] + jnp.sum(p, axis=0, keepdims=True)
                a_ref[:, cols] = alpha * a_ref[:, cols] + jnp.sum(p * d, axis=0, keepdims=True)

        return 0

    lax.fori_loop(0, NK, step, 0)
    l = l_ref[...]
    seen = l > 0.0
    safe = jnp.where(seen, l, 1.0)
    m_ref[...] = jnp.where(seen, m_ref[...] + jnp.log2(safe), FLOOR)
    a_ref[...] = jnp.where(seen, a_ref[...] / safe, 0.0)
    for c in range(STAT):
        cols = slice(c * HD, (c + 1) * HD)
        lse, delta = m_ref[:, cols], a_ref[:, cols]
        for i in range(NQ):
            st_ref[i, c : c + 1, :] = lse
            st_ref[i, STAT + c : STAT + c + 1, :] = delta


def stats(slots, kv):
    rows = jax.ShapeDtypeStruct((QL, HD), jnp.bfloat16)
    return pl.pallas_call(
        stats_kernel,
        in_specs=[vmem()] * 5,
        out_specs=[vmem()] * 5 + [smem()],
        out_shape=[
            jax.ShapeDtypeStruct((NQ, 2 * STAT, HD), jnp.float32),
            rows,
            rows,
            rows,
            rows,
            jax.ShapeDtypeStruct((64,), jnp.int32),
        ],
        scratch_shapes=[pltpu.VMEM((1, QL), jnp.float32)] * 3,
        compiler_params=pltpu.CompilerParams(vmem_limit_bytes=VMEM_LARGE),
        cost_estimate=pl.CostEstimate(flops=12 * 10**8, bytes_accessed=2 * 10**6, transcendentals=24 * 10**5),
        name="softmax_stats",
    )(*slots, kv)


def grad_kernel(perm_ref, qs_ref, gs_ref, ks_ref, vs_ref, st_ref, dkv_ref, keep_ref, send_ref, dqt_ref, lse_ref, delta_ref):
    ms = [st_ref[i, :STAT, :] for i in range(NQ)]
    m = functools.reduce(jnp.maximum, ms)
    w = [jnp.exp2(x - m) for x in ms]
    l = sum(w)
    lse = m + jnp.log2(l)
    delta = sum(w[i] * st_ref[i, STAT:, :] for i in range(NQ)) / l
    for c in range(STAT):
        lse_ref[:, c * HD : (c + 1) * HD] = lse[c : c + 1, :]
        delta_ref[:, c * HD : (c + 1) * HD] = delta[c : c + 1, :]
    dqt_ref[...] = jnp.zeros(dqt_ref.shape, jnp.float32)

    def step(pair, _):
        rows = block_rows(pair * TOK, TOK)
        tile = first_tile(perm_ref, pair)
        low, high = perm_ref[16 + 2 * pair], perm_ref[17 + 2 * pair]
        for first in range(NQ):

            @pl.when(tile == first)
            def _():
                cols = slice(first * QT, QL)
                k, q, g = ks_ref[rows, :], qs_ref[cols, :], gs_ref[cols, :]
                s = dot(k, q, 1, 1) * (SCALE * LOG2E)
                d = dot(vs_ref[rows, :], g, 1, 1)
                visible = key_positions(perm_ref, pair) <= query_positions(perm_ref, first)
                s = jnp.where(visible, s, FILL)
                p = jnp.exp2(s - lse_ref[:, cols])
                ds = (p * (d - delta_ref[:, cols])).astype(jnp.bfloat16)
                dv = dot(p.astype(jnp.bfloat16), g, 1, 0).astype(jnp.bfloat16)
                dk = dot(ds, q, 1, 0).astype(jnp.bfloat16)
                dqt_ref[:, cols] += dot(k, ds, 0, 0)
                dkv_ref[low, :, :HD] = dk[:BLOCK]
                dkv_ref[low, :, HD:] = dv[:BLOCK]
                dkv_ref[high, :, :HD] = dk[BLOCK:]
                dkv_ref[high, :, HD:] = dv[BLOCK:]

        @pl.when(tile == NQ)
        def _():
            empty = jnp.zeros((BLOCK, 2 * HD), jnp.bfloat16)
            dkv_ref[low] = empty
            dkv_ref[high] = empty

        return 0

    lax.fori_loop(0, NK, step, 0)
    for t in range(NQ):
        part = dqt_ref[:, t * QT : (t + 1) * QT].T
        for i in range(2):
            block = perm_ref[2 * t + i]
            both = jnp.concatenate(
                [part[(2 * i + head) * BLOCK : (2 * i + head + 1) * BLOCK] for head in range(2)], axis=1
            )

            @pl.when(block < NQ)
            def _():
                keep_ref[block] = both

            @pl.when(block >= NQ)
            def _():
                send_ref[block - NQ] = both


def grads(perm, qs, gs, ks, vs, st):
    half = jax.ShapeDtypeStruct((NQ, BLOCK, 2 * HD), jnp.float32)
    return pl.pallas_call(
        grad_kernel,
        in_specs=[smem()] + [vmem()] * 5,
        out_specs=[vmem()] * 3,
        out_shape=[jax.ShapeDtypeStruct((2 * NK, BLOCK, 2 * HD), jnp.bfloat16), half, half],
        scratch_shapes=[
            pltpu.VMEM((HD, QL), jnp.float32),
            pltpu.VMEM((1, QL), jnp.float32),
            pltpu.VMEM((1, QL), jnp.float32),
        ],
        compiler_params=pltpu.CompilerParams(vmem_limit_bytes=VMEM_LARGE),
        cost_estimate=pl.CostEstimate(flops=30 * 10**8, bytes_accessed=3 * 10**6, transcendentals=24 * 10**5),
        name="tile_gradients",
    )(perm, qs, gs, ks, vs, st)


def dq_kernel(a_ref, b_ref, c_ref, cs_ref, out_ref):
    for j in range(2):
        rows = slice(j * BLOCK, (j + 1) * BLOCK)
        cosine, sine = cs_ref[0, rows, :], cs_ref[1, rows, :]
        for head in range(2):
            cols = slice(head * HD, (head + 1) * HD)
            x = (a_ref[j, :, cols] + b_ref[j, :, cols] + c_ref[j, :, cols]) * SCALE
            out_ref[rows, cols] = (x * cosine - pltpu.roll(x, HD // 2, 1) * sine).astype(jnp.bfloat16)


def finish_dq(kept, near, far, cs):
    return pl.pallas_call(
        dq_kernel,
        in_specs=[vmem()] * 4,
        out_specs=vmem(),
        out_shape=jax.ShapeDtypeStruct((TOK, 2 * HD), jnp.bfloat16),
        compiler_params=pltpu.CompilerParams(vmem_limit_bytes=VMEM),
        cost_estimate=pl.CostEstimate(flops=10**6, bytes_accessed=10**6, transcendentals=0),
        name="query_gradient",
    )(kept, near, far, cs)


def square_kernel(yl_ref, parts_ref, cs_ref, out_ref):
    rows = pl.ds(pl.multiple_of(yl_ref[0] * BLOCK, BLOCK), BLOCK)
    cosine, sine = cs_ref[0, rows, :], cs_ref[1, rows, :]
    total = sum(parts_ref[i].astype(jnp.float32) for i in range(2 * NK))
    x = total[:, :HD] * SCALE
    y = total[:, HD:]
    x = x * cosine - pltpu.roll(x, HD // 2, 1) * sine
    x = jnp.sum(x * x, axis=0, keepdims=True)
    y = jnp.sum(y * y, axis=0, keepdims=True)
    out_ref[:, 0:1, :] = jnp.broadcast_to(x[None], (NALL, 1, HD))
    out_ref[:, 1:2, :] = jnp.broadcast_to(y[None], (NALL, 1, HD))


def squares(yl, parts, cs):
    return pl.pallas_call(
        square_kernel,
        in_specs=[smem(), vmem(), vmem()],
        out_specs=vmem(),
        out_shape=jax.ShapeDtypeStruct((NALL, 2, HD), jnp.float32),
        compiler_params=pltpu.CompilerParams(vmem_limit_bytes=VMEM),
        cost_estimate=pl.CostEstimate(flops=10**6, bytes_accessed=10**6, transcendentals=0),
        name="square_sums",
    )(yl, parts, cs)


def swap(value, axis):
    return lax.ppermute(value, axis, [(0, 1), (1, 0)])


def body(queries, keys, values, out_grad, positions):
    kvi = (lax.axis_index("xh") * 4 + lax.axis_index("yh")).astype(jnp.int32).reshape(1)
    yl = lax.axis_index("yl").astype(jnp.int32)
    freq = jnp.asarray(frequencies())
    kv, cs = prep_keys(kvi, positions, freq, keys, values)
    kv_all = lax.all_to_all(kv, AX_Z, 0, 0)
    qg = prep_queries(positions, cs, queries, out_grad)
    other_x = swap(qg, AX_X)
    other_core = swap(qg, AX_C)
    other_both = swap(other_x, AX_C)
    st, qs, gs, ks, vs, perm = stats((qg, other_x, other_core, other_both), kv_all)
    st_all = lax.all_to_all(st, QGROUP, 0, 0)
    dkv, keep, send = grads(perm, qs, gs, ks, vs, st_all)
    near = swap(send, AX_C)
    far = swap(keep[2:] + near[2:], AX_X)
    parts = lax.all_to_all(dkv, KGROUP, 0, 0)
    sums = lax.all_to_all(squares(yl.reshape(1), parts, cs), ALLGROUP, 0, 0)
    sums = jnp.sum(sums, axis=0)
    query_grad = finish_dq(keep[:2], near[:2], far, cs)
    mine = lax.dynamic_slice_in_dim(sums, yl * (HD // 2), HD // 2, 1) / SEQ
    return query_grad, mine[0:1], mine[1:2]


def solution(mesh):
    inner = Mesh(
        mesh.devices.reshape(8, 2, 2, 2, 4, 2), (AX_Z, AX_X, AX_C, "xh", "yh", "yl")
    )
    ctx, head = (AX_Z, AX_X, AX_C), ("xh", "yh", "yl")
    return jax.shard_map(
        body,
        mesh=inner,
        in_specs=(P(ctx, head), P(ctx, None), P(ctx, None), P(ctx, head), P(ctx)),
        out_specs=(P(ctx, head), P(head, None), P(head, None)),
        check_vma=False,
    )
```

```python
import functools
import math

import jax
import jax.numpy as jnp
import numpy as np
from jax import lax
from jax.experimental import pallas as pl
from jax.experimental.pallas import tpu as pltpu
from jax.sharding import Mesh
from jax.sharding import PartitionSpec as P

HD = 128
SEQ = 6144
BLOCK = 96
TOK = 192
PACK = TOK + 16
SCALE = HD ** (-0.5)
LOG2E = math.log2(math.e)
FILL = -1e30
FLOOR = -1e29
MIB = 1024 * 1024
VMEM = 20 * MIB
VMEM_LARGE = 32 * MIB
VMEM_ALL = 60 * MIB
ROWS = 2 * TOK + 16
AX_Z, AX_X, AX_C = "z", "xl", "core"
QGROUP = (AX_X, AX_C)
KGROUP = (AX_Z, "yl")
ALLGROUP = (AX_Z, AX_X, AX_C, "yl")
NQ = 4
NK = 8
NALL = 2 * NQ * NK
QL = 2 * NQ * TOK
STAT = QL // HD
QT = 384


def frequencies():
    half = HD // 2
    freq = np.float32(500000.0) ** (-(np.arange(half, dtype=np.float32) * np.float32(2.0) / np.float32(HD)))
    freq = freq.astype(np.float32)
    wave = (np.float32(2.0 * math.pi) / freq).astype(np.float32)
    smooth = np.clip((np.float32(8192.0) / wave - np.float32(1.0)) / np.float32(3.0), 0.0, 1.0).astype(np.float32)
    freq = (np.float32(1.0) - smooth) * freq / np.float32(8.0) + smooth * freq
    return np.concatenate([freq, freq]).astype(np.float32)[None, :]


def dot(a, b, ca, cb):
    return lax.dot_general(a, b, (((ca,), (cb,)), ((), ())), preferred_element_type=jnp.float32)


def smem():
    return pl.BlockSpec(memory_space=pltpu.SMEM)


def vmem():
    return pl.BlockSpec(memory_space=pltpu.VMEM)


def rotate(x, cosine, sine):
    x = x.astype(jnp.float32)
    return (x * cosine + pltpu.roll(x, HD // 2, 1) * sine).astype(jnp.bfloat16)


def id_rows(pos_ref, j):
    block = lax.div(pos_ref[j * BLOCK], BLOCK).astype(jnp.float32)
    return jnp.full((PACK - TOK, HD), block, jnp.float32).astype(jnp.bfloat16)


def key_kernel(kvi_ref, pos_ref, freq_ref, k_ref, v_ref, kv_ref, cs_ref):
    row = lax.broadcasted_iota(jnp.int32, (TOK, HD), 0)
    pos = jnp.where(row < BLOCK, pos_ref[0] + row, pos_ref[BLOCK] + row - BLOCK)
    angle = pos.astype(jnp.float32) * freq_ref[...]
    cosine = jnp.cos(angle)
    lane = lax.broadcasted_iota(jnp.int32, (TOK, HD), 1)
    sine = jnp.sin(angle)
    sine = jnp.where(lane < HD // 2, -sine, sine)
    cs_ref[0] = cosine
    cs_ref[1] = sine
    key = rotate(k_ref[...], cosine, sine)
    lanes = lax.broadcasted_iota(jnp.int32, (ROWS - 2 * TOK, HD), 1)
    first, second = (lax.div(pos_ref[j * BLOCK], BLOCK) for j in range(2))
    ids = jnp.where(lanes < HD // 2, first, second).astype(jnp.float32).astype(jnp.bfloat16)
    for i in range(NK):
        kv_ref[i, :TOK, :] = key
        kv_ref[i, TOK : 2 * TOK, :] = v_ref[...]
        kv_ref[i, 2 * TOK :, :] = ids


def prep_keys(kvi, positions, freq, keys, values):
    whole = lambda *shape: pl.BlockSpec(shape, lambda i, kvi, pos: (0,) * len(shape))
    picked = pl.BlockSpec((TOK, HD), lambda i, kvi, pos: (0, kvi[0]))
    return pl.pallas_call(
        key_kernel,
        grid_spec=pltpu.PrefetchScalarGridSpec(
            num_scalar_prefetch=2,
            grid=(1,),
            in_specs=[whole(1, HD), picked, picked],
            out_specs=[whole(NK, ROWS, HD), whole(2, TOK, HD)],
        ),
        out_shape=[
            jax.ShapeDtypeStruct((NK, ROWS, HD), jnp.bfloat16),
            jax.ShapeDtypeStruct((2, TOK, HD), jnp.float32),
        ],
        compiler_params=pltpu.CompilerParams(vmem_limit_bytes=VMEM_ALL),
        cost_estimate=pl.CostEstimate(flops=10**6, bytes_accessed=10**6, transcendentals=10**5),
        name="rotate_keys",
    )(kvi, positions, freq, keys, values)


def query_kernel(pos_ref, cs_ref, q_ref, g_ref, qg_ref):
    for head in range(2):
        cols = slice(head * HD, (head + 1) * HD)
        qg_ref[:TOK, cols] = rotate(q_ref[:, cols], cs_ref[0], cs_ref[1])
    qg_ref[:TOK, 2 * HD :] = g_ref[...]
    for j in range(4):
        qg_ref[TOK:, j * HD : (j + 1) * HD] = id_rows(pos_ref, j % 2)


def prep_queries(positions, cs, queries, out_grad):
    return pl.pallas_call(
        query_kernel,
        in_specs=[smem()] + [vmem()] * 3,
        out_specs=vmem(),
        out_shape=jax.ShapeDtypeStruct((PACK, 4 * HD), jnp.bfloat16),
        compiler_params=pltpu.CompilerParams(vmem_limit_bytes=VMEM),
        cost_estimate=pl.CostEstimate(flops=10**6, bytes_accessed=10**6, transcendentals=0),
        name="rotate_queries",
    )(positions, cs, queries, out_grad)


def block_id(ref, column):
    rows = ref[TOK:PACK, column * HD : (column + 1) * HD]
    return jnp.max(rows.astype(jnp.float32)).astype(jnp.int32)


def key_ids(kv_ref, c):
    rows = kv_ref[c, 2 * TOK :, :].astype(jnp.float32)
    lanes = lax.broadcasted_iota(jnp.int32, rows.shape, 1)
    masked = (jnp.where(lanes < HD // 2, rows, 0.0), jnp.where(lanes < HD // 2, 0.0, rows))
    return [jnp.max(x).astype(jnp.int32) for x in masked]


def ranks_of(ids):
    count = len(ids)
    return [sum((ids[i] < ids[j]).astype(jnp.int32) for i in range(count) if i != j) for j in range(count)]


def query_positions(perm_ref, first):
    lane = lax.broadcasted_iota(jnp.int32, (1, QL - first * QT), 1)
    pos = jnp.zeros(lane.shape, jnp.int32)
    for r in range(2 * first, 2 * NQ):
        for head in range(2):
            start = (r - 2 * first) * TOK + head * BLOCK
            pos = jnp.where(lane >= start, perm_ref[8 + r] * BLOCK - start + lane, pos)
    return pos


def key_positions(perm_ref, pair):
    row = lax.broadcasted_iota(jnp.int32, (TOK, 1), 0)
    low, high = perm_ref[32 + 2 * pair], perm_ref[33 + 2 * pair]
    return row + jnp.where(row < BLOCK, low * BLOCK, (high - 1) * BLOCK)


def first_tile(perm_ref, pair):
    low = perm_ref[32 + 2 * pair]
    return sum((perm_ref[9 + 2 * t] < low).astype(jnp.int32) for t in range(NQ))


def block_rows(start, count):
    return pl.ds(pl.multiple_of(start, BLOCK), count)


def sort_kernel(q0, q1, q2, q3, qs_ref, gs_ref, qpos_ref, perm_ref):
    slots = (q0, q1, q2, q3)
    ids = [block_id(ref, j) for ref in slots for j in range(2)]
    for j, r in enumerate(ranks_of(ids)):
        perm_ref[r] = j
        perm_ref[8 + r] = ids[j]
        ref, rows = slots[j // 2], slice((j % 2) * BLOCK, (j % 2 + 1) * BLOCK)
        for head in range(2):
            to = block_rows(r * TOK + head * BLOCK, BLOCK)
            qs_ref[to, :] = ref[rows, head * HD : (head + 1) * HD]
            gs_ref[to, :] = ref[rows, (2 + head) * HD : (3 + head) * HD]
    qpos_ref[...] = query_positions(perm_ref, 0)


def sort_queries(slots):
    rows = jax.ShapeDtypeStruct((QL, HD), jnp.bfloat16)
    return pl.pallas_call(
        sort_kernel,
        in_specs=[vmem()] * 4,
        out_specs=[vmem()] * 3 + [smem()],
        out_shape=[
            rows,
            rows,
            jax.ShapeDtypeStruct((1, QL), jnp.int32),
            jax.ShapeDtypeStruct((16,), jnp.int32),
        ],
        compiler_params=pltpu.CompilerParams(vmem_limit_bytes=VMEM),
        cost_estimate=pl.CostEstimate(flops=10**6, bytes_accessed=10**6, transcendentals=0),
        name="sort_queries",
    )(*slots)


def stats_kernel(
    order_ref, qs_ref, gs_ref, qpos_ref, kv_ref, st_ref, ks_ref, s_ref, d_ref, perm_ref, vs_ref, m_ref, l_ref, a_ref
):
    for j in range(16):
        perm_ref[j] = order_ref[j]
    ids = [x for c in range(NK) for x in key_ids(kv_ref, c)]
    for j, r in enumerate(ranks_of(ids)):
        perm_ref[16 + r] = j
        perm_ref[32 + r] = ids[j]
        rows = slice((j % 2) * BLOCK, (j % 2 + 1) * BLOCK)
        to = block_rows(r * BLOCK, BLOCK)
        ks_ref[to, :] = kv_ref[j // 2, rows, :]
        vs_ref[to, :] = kv_ref[j // 2, slice(TOK + rows.start, TOK + rows.stop), :]
    m_ref[...] = jnp.full(m_ref.shape, FLOOR, jnp.float32)
    l_ref[...] = jnp.zeros(l_ref.shape, jnp.float32)
    a_ref[...] = jnp.zeros(a_ref.shape, jnp.float32)

    def step(pair, _):
        rows = block_rows(pair * TOK, TOK)
        tile = first_tile(perm_ref, pair)
        for first in range(NQ):

            @pl.when(tile == first)
            def _():
                cols = slice(first * QT, QL)
                s = dot(ks_ref[rows, :], qs_ref[cols, :], 1, 1) * (SCALE * LOG2E)
                d = dot(vs_ref[rows, :], gs_ref[cols, :], 1, 1)
                s = jnp.where(key_positions(perm_ref, pair) <= qpos_ref[:, cols], s, FILL)
                s_ref[pair, :, cols] = s
                d_ref[pair, :, cols] = d
                m = m_ref[:, cols]
                m2 = jnp.maximum(m, jnp.max(s, axis=0, keepdims=True))
                p = jnp.exp2(s - m2)
                alpha = jnp.exp2(m - m2)
                m_ref[:, cols] = m2
                l_ref[:, cols] = alpha * l_ref[:, cols] + jnp.sum(p, axis=0, keepdims=True)
                a_ref[:, cols] = alpha * a_ref[:, cols] + jnp.sum(p * d, axis=0, keepdims=True)

        return 0

    lax.fori_loop(0, NK, step, 0)
    l = l_ref[...]
    seen = l > 0.0
    safe = jnp.where(seen, l, 1.0)
    m_ref[...] = jnp.where(seen, m_ref[...] + jnp.log2(safe), FLOOR)
    a_ref[...] = jnp.where(seen, a_ref[...] / safe, 0.0)
    for c in range(STAT):
        cols = slice(c * HD, (c + 1) * HD)
        lse, delta = m_ref[:, cols], a_ref[:, cols]
        for i in range(NQ):
            st_ref[i, c : c + 1, :] = lse
            st_ref[i, STAT + c : STAT + c + 1, :] = delta


def stats(order, qs, gs, qpos, kv):
    products = jax.ShapeDtypeStruct((NK, TOK, QL), jnp.float32)
    return pl.pallas_call(
        stats_kernel,
        in_specs=[smem()] + [vmem()] * 4,
        out_specs=[vmem()] * 4 + [smem()],
        out_shape=[
            jax.ShapeDtypeStruct((NQ, 2 * STAT, HD), jnp.float32),
            jax.ShapeDtypeStruct((NK * TOK, HD), jnp.bfloat16),
            products,
            products,
            jax.ShapeDtypeStruct((64,), jnp.int32),
        ],
        scratch_shapes=[pltpu.VMEM((NK * TOK, HD), jnp.bfloat16)] + [pltpu.VMEM((1, QL), jnp.float32)] * 3,
        compiler_params=pltpu.CompilerParams(vmem_limit_bytes=VMEM_LARGE),
        cost_estimate=pl.CostEstimate(flops=12 * 10**8, bytes_accessed=2 * 10**6, transcendentals=24 * 10**5),
        name="softmax_stats",
    )(order, qs, gs, qpos, kv)


def grad_kernel(perm_ref, qs_ref, gs_ref, ks_ref, s_ref, d_ref, st_ref, dkv_ref, keep_ref, send_ref, dqt_ref, lse_ref, delta_ref):
    ms = [st_ref[i, :STAT, :] for i in range(NQ)]
    m = functools.reduce(jnp.maximum, ms)
    w = [jnp.exp2(x - m) for x in ms]
    l = sum(w)
    lse = m + jnp.log2(l)
    delta = sum(w[i] * st_ref[i, STAT:, :] for i in range(NQ)) / l
    for c in range(STAT):
        lse_ref[:, c * HD : (c + 1) * HD] = lse[c : c + 1, :]
        delta_ref[:, c * HD : (c + 1) * HD] = delta[c : c + 1, :]
    dqt_ref[...] = jnp.zeros(dqt_ref.shape, jnp.float32)

    def step(pair, _):
        rows = block_rows(pair * TOK, TOK)
        tile = first_tile(perm_ref, pair)
        low, high = perm_ref[16 + 2 * pair], perm_ref[17 + 2 * pair]
        for first in range(NQ):

            @pl.when(tile == first)
            def _():
                cols = slice(first * QT, QL)
                k, q, g = ks_ref[rows, :], qs_ref[cols, :], gs_ref[cols, :]
                p = jnp.exp2(s_ref[pair, :, cols] - lse_ref[:, cols])
                ds = (p * (d_ref[pair, :, cols] - delta_ref[:, cols])).astype(jnp.bfloat16)
                dv = dot(p.astype(jnp.bfloat16), g, 1, 0).astype(jnp.bfloat16)
                dk = dot(ds, q, 1, 0).astype(jnp.bfloat16)
                dqt_ref[:, cols] += dot(k, ds, 0, 0)
                dkv_ref[low, :, :HD] = dk[:BLOCK]
                dkv_ref[low, :, HD:] = dv[:BLOCK]
                dkv_ref[high, :, :HD] = dk[BLOCK:]
                dkv_ref[high, :, HD:] = dv[BLOCK:]

        @pl.when(tile == NQ)
        def _():
            empty = jnp.zeros((BLOCK, 2 * HD), jnp.bfloat16)
            dkv_ref[low] = empty
            dkv_ref[high] = empty

        return 0

    lax.fori_loop(0, NK, step, 0)
    for t in range(NQ):
        part = dqt_ref[:, t * QT : (t + 1) * QT].T
        for i in range(2):
            block = perm_ref[2 * t + i]
            both = jnp.concatenate(
                [part[(2 * i + head) * BLOCK : (2 * i + head + 1) * BLOCK] for head in range(2)], axis=1
            )

            @pl.when(block < NQ)
            def _():
                keep_ref[block] = both

            @pl.when(block >= NQ)
            def _():
                send_ref[block - NQ] = both


def grads(perm, qs, gs, ks, s, d, st):
    half = jax.ShapeDtypeStruct((NQ, BLOCK, 2 * HD), jnp.float32)
    return pl.pallas_call(
        grad_kernel,
        in_specs=[smem()] + [vmem()] * 6,
        out_specs=[vmem()] * 3,
        out_shape=[jax.ShapeDtypeStruct((2 * NK, BLOCK, 2 * HD), jnp.bfloat16), half, half],
        scratch_shapes=[
            pltpu.VMEM((HD, QL), jnp.float32),
            pltpu.VMEM((1, QL), jnp.float32),
            pltpu.VMEM((1, QL), jnp.float32),
        ],
        compiler_params=pltpu.CompilerParams(vmem_limit_bytes=VMEM_LARGE),
        cost_estimate=pl.CostEstimate(flops=30 * 10**8, bytes_accessed=3 * 10**6, transcendentals=24 * 10**5),
        name="tile_gradients",
    )(perm, qs, gs, ks, s, d, st)


def dq_kernel(a_ref, b_ref, c_ref, cs_ref, out_ref):
    for j in range(2):
        rows = slice(j * BLOCK, (j + 1) * BLOCK)
        cosine, sine = cs_ref[0, rows, :], cs_ref[1, rows, :]
        for head in range(2):
            cols = slice(head * HD, (head + 1) * HD)
            x = (a_ref[j, :, cols] + b_ref[j, :, cols] + c_ref[j, :, cols]) * SCALE
            out_ref[rows, cols] = (x * cosine - pltpu.roll(x, HD // 2, 1) * sine).astype(jnp.bfloat16)


def finish_dq(kept, near, far, cs):
    return pl.pallas_call(
        dq_kernel,
        in_specs=[vmem()] * 4,
        out_specs=vmem(),
        out_shape=jax.ShapeDtypeStruct((TOK, 2 * HD), jnp.bfloat16),
        compiler_params=pltpu.CompilerParams(vmem_limit_bytes=VMEM),
        cost_estimate=pl.CostEstimate(flops=10**6, bytes_accessed=10**6, transcendentals=0),
        name="query_gradient",
    )(kept, near, far, cs)


def square_kernel(yl_ref, parts_ref, cs_ref, out_ref):
    rows = pl.ds(pl.multiple_of(yl_ref[0] * BLOCK, BLOCK), BLOCK)
    cosine, sine = cs_ref[0, rows, :], cs_ref[1, rows, :]
    total = sum(parts_ref[i].astype(jnp.float32) for i in range(2 * NK))
    x = total[:, :HD] * SCALE
    y = total[:, HD:]
    x = x * cosine - pltpu.roll(x, HD // 2, 1) * sine
    x = jnp.sum(x * x, axis=0, keepdims=True)
    y = jnp.sum(y * y, axis=0, keepdims=True)
    out_ref[:, 0:1, :] = jnp.broadcast_to(x[None], (NALL, 1, HD))
    out_ref[:, 1:2, :] = jnp.broadcast_to(y[None], (NALL, 1, HD))


def squares(yl, parts, cs):
    return pl.pallas_call(
        square_kernel,
        in_specs=[smem(), vmem(), vmem()],
        out_specs=vmem(),
        out_shape=jax.ShapeDtypeStruct((NALL, 2, HD), jnp.float32),
        compiler_params=pltpu.CompilerParams(vmem_limit_bytes=VMEM),
        cost_estimate=pl.CostEstimate(flops=10**6, bytes_accessed=10**6, transcendentals=0),
        name="square_sums",
    )(yl, parts, cs)


def swap(value, axis):
    return lax.ppermute(value, axis, [(0, 1), (1, 0)])


def body(queries, keys, values, out_grad, positions):
    kvi = (lax.axis_index("xh") * 4 + lax.axis_index("yh")).astype(jnp.int32).reshape(1)
    yl = lax.axis_index("yl").astype(jnp.int32)
    freq = jnp.asarray(frequencies())
    kv, cs = prep_keys(kvi, positions, freq, keys, values)
    kv_all = lax.all_to_all(kv, AX_Z, 0, 0)
    qg = prep_queries(positions, cs, queries, out_grad)
    other_x = swap(qg, AX_X)
    other_core = swap(qg, AX_C)
    other_both = swap(other_x, AX_C)
    qs, gs, qpos, order = sort_queries((qg, other_x, other_core, other_both))
    st, ks, s, d, perm = stats(order, qs, gs, qpos, kv_all)
    st_all = lax.all_to_all(st, QGROUP, 0, 0)
    dkv, keep, send = grads(perm, qs, gs, ks, s, d, st_all)
    near = swap(send, AX_C)
    far = swap(keep[2:] + near[2:], AX_X)
    parts = lax.all_to_all(dkv, KGROUP, 0, 0)
    sums = lax.all_to_all(squares(yl.reshape(1), parts, cs), ALLGROUP, 0, 0)
    sums = jnp.sum(sums, axis=0)
    query_grad = finish_dq(keep[:2], near[:2], far, cs)
    mine = lax.dynamic_slice_in_dim(sums, yl * (HD // 2), HD // 2, 1) / SEQ
    return query_grad, mine[0:1], mine[1:2]


def solution(mesh):
    inner = Mesh(
        mesh.devices.reshape(8, 2, 2, 2, 4, 2), (AX_Z, AX_X, AX_C, "xh", "yh", "yl")
    )
    ctx, head = (AX_Z, AX_X, AX_C), ("xh", "yh", "yl")
    return jax.shard_map(
        body,
        mesh=inner,
        in_specs=(P(ctx, head), P(ctx, None), P(ctx, None), P(ctx, head), P(ctx)),
        out_specs=(P(ctx, head), P(head, None), P(head, None)),
        check_vma=False,
    )
```

```python
import functools
import math

import jax
import jax.numpy as jnp
import numpy as np
from jax import lax
from jax.experimental import pallas as pl
from jax.experimental.pallas import tpu as pltpu
from jax.sharding import Mesh
from jax.sharding import PartitionSpec as P

HD = 128
SEQ = 6144
BLOCK = 96
TOK = 192
PACK = TOK + 16
SCALE = HD ** (-0.5)
LOG2E = math.log2(math.e)
FILL = -1e30
FLOOR = -1e29
MIB = 1024 * 1024
VMEM = 20 * MIB
VMEM_LARGE = 32 * MIB
VMEM_ALL = 60 * MIB
VMEM_GRADS = 32 * MIB
ROWS = 2 * TOK + 16
AX_Z, AX_X, AX_C = "z", "xl", "core"
QGROUP = (AX_X, AX_C)
KGROUP = (AX_Z, "yl")
ALLGROUP = (AX_Z, AX_X, AX_C, "yl")
NQ = 4
NK = 8
NALL = 2 * NQ * NK
QL = 2 * NQ * TOK
STAT = QL // HD
QT = 384


def frequencies():
    half = HD // 2
    freq = np.float32(500000.0) ** (-(np.arange(half, dtype=np.float32) * np.float32(2.0) / np.float32(HD)))
    freq = freq.astype(np.float32)
    wave = (np.float32(2.0 * math.pi) / freq).astype(np.float32)
    smooth = np.clip((np.float32(8192.0) / wave - np.float32(1.0)) / np.float32(3.0), 0.0, 1.0).astype(np.float32)
    freq = (np.float32(1.0) - smooth) * freq / np.float32(8.0) + smooth * freq
    return np.concatenate([freq, freq]).astype(np.float32)[None, :]


def dot(a, b, ca, cb):
    return lax.dot_general(a, b, (((ca,), (cb,)), ((), ())), preferred_element_type=jnp.float32)


def smem():
    return pl.BlockSpec(memory_space=pltpu.SMEM)


def vmem():
    return pl.BlockSpec(memory_space=pltpu.VMEM)


def rotate(x, cosine, sine):
    x = x.astype(jnp.float32)
    return (x * cosine + pltpu.roll(x, HD // 2, 1) * sine).astype(jnp.bfloat16)


def id_rows(pos_ref, j):
    block = lax.div(pos_ref[j * BLOCK], BLOCK).astype(jnp.float32)
    return jnp.full((PACK - TOK, HD), block, jnp.float32).astype(jnp.bfloat16)


def key_kernel(kvi_ref, pos_ref, freq_ref, k_ref, v_ref, kv_ref, cs_ref):
    row = lax.broadcasted_iota(jnp.int32, (BLOCK, HD), 0)
    lane = lax.broadcasted_iota(jnp.int32, (BLOCK, HD), 1)
    lower = lane < HD // 2
    angle = (row + jnp.where(lower, pos_ref[0], pos_ref[BLOCK])).astype(jnp.float32) * freq_ref[...]

    def spread(packed):
        other = pltpu.roll(packed, HD // 2, 1)
        return jnp.where(lower, packed, other), jnp.where(lower, other, packed)

    for j, (c, s) in enumerate(zip(spread(jnp.cos(angle)), spread(jnp.sin(angle)))):
        cs_ref[0, j * BLOCK : (j + 1) * BLOCK, :] = c
        cs_ref[1, j * BLOCK : (j + 1) * BLOCK, :] = jnp.where(lower, -s, s)
    cosine, sine = cs_ref[0], cs_ref[1]
    key = rotate(k_ref[...], cosine, sine)
    lanes = lax.broadcasted_iota(jnp.int32, (ROWS - 2 * TOK, HD), 1)
    first, second = (lax.div(pos_ref[j * BLOCK], BLOCK) for j in range(2))
    ids = jnp.where(lanes < HD // 2, first, second).astype(jnp.float32).astype(jnp.bfloat16)
    for i in range(NK):
        kv_ref[i, :TOK, :] = key
        kv_ref[i, TOK : 2 * TOK, :] = v_ref[...]
        kv_ref[i, 2 * TOK :, :] = ids


def prep_keys(kvi, positions, freq, keys, values):
    whole = lambda *shape: pl.BlockSpec(shape, lambda i, kvi, pos: (0,) * len(shape))
    picked = pl.BlockSpec((TOK, HD), lambda i, kvi, pos: (0, kvi[0]))
    return pl.pallas_call(
        key_kernel,
        grid_spec=pltpu.PrefetchScalarGridSpec(
            num_scalar_prefetch=2,
            grid=(1,),
            in_specs=[whole(1, HD), picked, picked],
            out_specs=[whole(NK, ROWS, HD), whole(2, TOK, HD)],
        ),
        out_shape=[
            jax.ShapeDtypeStruct((NK, ROWS, HD), jnp.bfloat16),
            jax.ShapeDtypeStruct((2, TOK, HD), jnp.float32),
        ],
        compiler_params=pltpu.CompilerParams(vmem_limit_bytes=VMEM_ALL),
        cost_estimate=pl.CostEstimate(flops=10**6, bytes_accessed=10**6, transcendentals=10**5),
        name="rotate_keys",
    )(kvi, positions, freq, keys, values)


def query_kernel(pos_ref, cs_ref, q_ref, g_ref, qg_ref):
    for head in range(2):
        cols = slice(head * HD, (head + 1) * HD)
        qg_ref[:TOK, cols] = rotate(q_ref[:, cols], cs_ref[0], cs_ref[1])
    qg_ref[:TOK, 2 * HD :] = g_ref[...]
    for j in range(4):
        qg_ref[TOK:, j * HD : (j + 1) * HD] = id_rows(pos_ref, j % 2)


def prep_queries(positions, cs, queries, out_grad):
    return pl.pallas_call(
        query_kernel,
        in_specs=[smem()] + [vmem()] * 3,
        out_specs=vmem(),
        out_shape=jax.ShapeDtypeStruct((PACK, 4 * HD), jnp.bfloat16),
        compiler_params=pltpu.CompilerParams(vmem_limit_bytes=VMEM),
        cost_estimate=pl.CostEstimate(flops=10**6, bytes_accessed=10**6, transcendentals=0),
        name="rotate_queries",
    )(positions, cs, queries, out_grad)


def block_id(ref, column):
    rows = ref[TOK:PACK, column * HD : (column + 1) * HD]
    return jnp.max(rows.astype(jnp.float32)).astype(jnp.int32)


def key_ids(kv_ref, c):
    rows = kv_ref[c, 2 * TOK :, :].astype(jnp.float32)
    lanes = lax.broadcasted_iota(jnp.int32, rows.shape, 1)
    masked = (jnp.where(lanes < HD // 2, rows, 0.0), jnp.where(lanes < HD // 2, 0.0, rows))
    return [jnp.max(x).astype(jnp.int32) for x in masked]


def ranks_of(ids):
    count = len(ids)
    return [sum((ids[i] < ids[j]).astype(jnp.int32) for i in range(count) if i != j) for j in range(count)]


def query_positions(perm_ref, first):
    lane = lax.broadcasted_iota(jnp.int32, (1, QL - first * QT), 1)
    pos = jnp.zeros(lane.shape, jnp.int32)
    for r in range(2 * first, 2 * NQ):
        for head in range(2):
            start = (r - 2 * first) * TOK + head * BLOCK
            pos = jnp.where(lane >= start, perm_ref[8 + r] * BLOCK - start + lane, pos)
    return pos


def key_positions(perm_ref, pair):
    row = lax.broadcasted_iota(jnp.int32, (TOK, 1), 0)
    low, high = perm_ref[32 + 2 * pair], perm_ref[33 + 2 * pair]
    return row + jnp.where(row < BLOCK, low * BLOCK, (high - 1) * BLOCK)


def first_tile(perm_ref, pair):
    low = perm_ref[32 + 2 * pair]
    return sum((perm_ref[9 + 2 * t] < low).astype(jnp.int32) for t in range(NQ))


def block_rows(start, count):
    return pl.ds(pl.multiple_of(start, BLOCK), count)


def sort_kernel(q0, q1, q2, q3, qs_ref, gs_ref, qpos_ref, perm_ref):
    slots = (q0, q1, q2, q3)
    ids = [block_id(ref, j) for ref in slots for j in range(2)]
    for j, r in enumerate(ranks_of(ids)):
        perm_ref[r] = j
        perm_ref[8 + r] = ids[j]
        ref, rows = slots[j // 2], slice((j % 2) * BLOCK, (j % 2 + 1) * BLOCK)
        for head in range(2):
            to = block_rows(r * TOK + head * BLOCK, BLOCK)
            qs_ref[to, :] = ref[rows, head * HD : (head + 1) * HD]
            gs_ref[to, :] = ref[rows, (2 + head) * HD : (3 + head) * HD]
    qpos_ref[...] = query_positions(perm_ref, 0)


def sort_queries(slots):
    rows = jax.ShapeDtypeStruct((QL, HD), jnp.bfloat16)
    return pl.pallas_call(
        sort_kernel,
        in_specs=[vmem()] * 4,
        out_specs=[vmem()] * 3 + [smem()],
        out_shape=[
            rows,
            rows,
            jax.ShapeDtypeStruct((1, QL), jnp.int32),
            jax.ShapeDtypeStruct((16,), jnp.int32),
        ],
        compiler_params=pltpu.CompilerParams(vmem_limit_bytes=VMEM),
        cost_estimate=pl.CostEstimate(flops=10**6, bytes_accessed=10**6, transcendentals=0),
        name="sort_queries",
    )(*slots)


def stats_kernel(
    order_ref, qs_ref, gs_ref, qpos_ref, kv_ref, st_ref, ks_ref, s_ref, d_ref, perm_ref, vs_ref, m_ref, l_ref, a_ref
):
    for j in range(16):
        perm_ref[j] = order_ref[j]
    ids = [x for c in range(NK) for x in key_ids(kv_ref, c)]
    for j, r in enumerate(ranks_of(ids)):
        perm_ref[16 + r] = j
        perm_ref[32 + r] = ids[j]
        rows = slice((j % 2) * BLOCK, (j % 2 + 1) * BLOCK)
        to = block_rows(r * BLOCK, BLOCK)
        ks_ref[to, :] = kv_ref[j // 2, rows, :]
        vs_ref[to, :] = kv_ref[j // 2, slice(TOK + rows.start, TOK + rows.stop), :]
    m_ref[...] = jnp.full(m_ref.shape, FLOOR, jnp.float32)
    l_ref[...] = jnp.zeros(l_ref.shape, jnp.float32)
    a_ref[...] = jnp.zeros(a_ref.shape, jnp.float32)

    def step(pair, _):
        rows = block_rows(pair * TOK, TOK)
        tile = first_tile(perm_ref, pair)
        for first in range(NQ):

            @pl.when(tile == first)
            def _():
                cols = slice(first * QT, QL)
                s = dot(ks_ref[rows, :], qs_ref[cols, :], 1, 1) * (SCALE * LOG2E)
                d = dot(vs_ref[rows, :], gs_ref[cols, :], 1, 1)
                s = jnp.where(key_positions(perm_ref, pair) <= qpos_ref[:, cols], s, FILL)
                s_ref[pair, :, cols] = s
                d_ref[pair, :, cols] = d
                m = m_ref[:, cols]
                m2 = jnp.maximum(m, jnp.max(s, axis=0, keepdims=True))
                p = jnp.exp2(s - m2)
                alpha = jnp.exp2(m - m2)
                m_ref[:, cols] = m2
                l_ref[:, cols] = alpha * l_ref[:, cols] + jnp.sum(p, axis=0, keepdims=True)
                a_ref[:, cols] = alpha * a_ref[:, cols] + jnp.sum(p * d, axis=0, keepdims=True)

        return 0

    lax.fori_loop(0, NK, step, 0)
    l = l_ref[...]
    seen = l > 0.0
    safe = jnp.where(seen, l, 1.0)
    m_ref[...] = jnp.where(seen, m_ref[...] + jnp.log2(safe), FLOOR)
    a_ref[...] = jnp.where(seen, a_ref[...] / safe, 0.0)
    for c in range(STAT):
        cols = slice(c * HD, (c + 1) * HD)
        lse, delta = m_ref[:, cols], a_ref[:, cols]
        for i in range(NQ):
            st_ref[i, c : c + 1, :] = lse
            st_ref[i, STAT + c : STAT + c + 1, :] = delta


def stats(order, qs, gs, qpos, kv):
    products = jax.ShapeDtypeStruct((NK, TOK, QL), jnp.float32)
    return pl.pallas_call(
        stats_kernel,
        in_specs=[smem()] + [vmem()] * 4,
        out_specs=[vmem()] * 4 + [smem()],
        out_shape=[
            jax.ShapeDtypeStruct((NQ, 2 * STAT, HD), jnp.float32),
            jax.ShapeDtypeStruct((NK * TOK, HD), jnp.bfloat16),
            products,
            products,
            jax.ShapeDtypeStruct((64,), jnp.int32),
        ],
        scratch_shapes=[pltpu.VMEM((NK * TOK, HD), jnp.bfloat16)] + [pltpu.VMEM((1, QL), jnp.float32)] * 3,
        compiler_params=pltpu.CompilerParams(vmem_limit_bytes=VMEM_LARGE),
        cost_estimate=pl.CostEstimate(flops=12 * 10**8, bytes_accessed=2 * 10**6, transcendentals=24 * 10**5),
        name="softmax_stats",
    )(order, qs, gs, qpos, kv)


def grad_kernel(perm_ref, qs_ref, gs_ref, ks_ref, s_ref, d_ref, st_ref, dkv_ref, keep_ref, send_ref, dqt_ref, lse_ref, delta_ref):
    ms = [st_ref[i, :STAT, :] for i in range(NQ)]
    m = functools.reduce(jnp.maximum, ms)
    w = [jnp.exp2(x - m) for x in ms]
    l = sum(w)
    lse = m + jnp.log2(l)
    delta = sum(w[i] * st_ref[i, STAT:, :] for i in range(NQ)) / l
    for c in range(STAT):
        lse_ref[:, c * HD : (c + 1) * HD] = lse[c : c + 1, :]
        delta_ref[:, c * HD : (c + 1) * HD] = delta[c : c + 1, :]
    dqt_ref[...] = jnp.zeros(dqt_ref.shape, jnp.float32)

    def step(pair, _):
        rows = block_rows(pair * TOK, TOK)
        tile = first_tile(perm_ref, pair)
        low, high = perm_ref[16 + 2 * pair], perm_ref[17 + 2 * pair]
        for first in range(NQ):

            @pl.when(tile == first)
            def _():
                cols = slice(first * QT, QL)
                k, q, g = ks_ref[rows, :], qs_ref[cols, :], gs_ref[cols, :]
                p = jnp.exp2(s_ref[pair, :, cols] - lse_ref[:, cols])
                ds = (p * (d_ref[pair, :, cols] - delta_ref[:, cols])).astype(jnp.bfloat16)
                dv = dot(p.astype(jnp.bfloat16), g, 1, 0).astype(jnp.bfloat16)
                dk = dot(ds, q, 1, 0).astype(jnp.bfloat16)
                dqt_ref[:, cols] += dot(k, ds, 0, 0)
                dkv_ref[low, :, :HD] = dk[:BLOCK]
                dkv_ref[low, :, HD:] = dv[:BLOCK]
                dkv_ref[high, :, :HD] = dk[BLOCK:]
                dkv_ref[high, :, HD:] = dv[BLOCK:]

        @pl.when(tile == NQ)
        def _():
            empty = jnp.zeros((BLOCK, 2 * HD), jnp.bfloat16)
            dkv_ref[low] = empty
            dkv_ref[high] = empty

        return 0

    lax.fori_loop(0, NK, step, 0)
    for t in range(NQ):
        part = dqt_ref[:, t * QT : (t + 1) * QT].T
        for i in range(2):
            block = perm_ref[2 * t + i]
            both = jnp.concatenate(
                [part[(2 * i + head) * BLOCK : (2 * i + head + 1) * BLOCK] for head in range(2)], axis=1
            )

            @pl.when(block < NQ)
            def _():
                keep_ref[block] = both

            @pl.when(block >= NQ)
            def _():
                send_ref[block - NQ] = both


def grads(perm, qs, gs, ks, s, d, st):
    half = jax.ShapeDtypeStruct((NQ, BLOCK, 2 * HD), jnp.float32)
    return pl.pallas_call(
        grad_kernel,
        in_specs=[smem()] + [vmem()] * 6,
        out_specs=[vmem()] * 3,
        out_shape=[jax.ShapeDtypeStruct((2 * NK, BLOCK, 2 * HD), jnp.bfloat16), half, half],
        scratch_shapes=[
            pltpu.VMEM((HD, QL), jnp.float32),
            pltpu.VMEM((1, QL), jnp.float32),
            pltpu.VMEM((1, QL), jnp.float32),
        ],
        compiler_params=pltpu.CompilerParams(vmem_limit_bytes=VMEM_GRADS),
        cost_estimate=pl.CostEstimate(flops=30 * 10**8, bytes_accessed=3 * 10**6, transcendentals=24 * 10**5),
        name="tile_gradients",
    )(perm, qs, gs, ks, s, d, st)


def dq_kernel(a_ref, b_ref, c_ref, cs_ref, out_ref):
    for j in range(2):
        rows = slice(j * BLOCK, (j + 1) * BLOCK)
        cosine, sine = cs_ref[0, rows, :], cs_ref[1, rows, :]
        for head in range(2):
            cols = slice(head * HD, (head + 1) * HD)
            x = (a_ref[j, :, cols] + b_ref[j, :, cols] + c_ref[j, :, cols]) * SCALE
            out_ref[rows, cols] = (x * cosine - pltpu.roll(x, HD // 2, 1) * sine).astype(jnp.bfloat16)


def finish_dq(kept, near, far, cs):
    return pl.pallas_call(
        dq_kernel,
        in_specs=[vmem()] * 4,
        out_specs=vmem(),
        out_shape=jax.ShapeDtypeStruct((TOK, 2 * HD), jnp.bfloat16),
        compiler_params=pltpu.CompilerParams(vmem_limit_bytes=VMEM),
        cost_estimate=pl.CostEstimate(flops=10**6, bytes_accessed=10**6, transcendentals=0),
        name="query_gradient",
    )(kept, near, far, cs)


def square_kernel(yl_ref, parts_ref, cs_ref, out_ref):
    rows = pl.ds(pl.multiple_of(yl_ref[0] * BLOCK, BLOCK), BLOCK)
    cosine, sine = cs_ref[0, rows, :], cs_ref[1, rows, :]
    total = sum(parts_ref[i].astype(jnp.float32) for i in range(2 * NK))
    x = total[:, :HD] * SCALE
    y = total[:, HD:]
    x = x * cosine - pltpu.roll(x, HD // 2, 1) * sine
    x = jnp.sum(x * x, axis=0, keepdims=True)
    y = jnp.sum(y * y, axis=0, keepdims=True)
    out_ref[:, 0:1, :] = jnp.broadcast_to(x[None], (NALL, 1, HD))
    out_ref[:, 1:2, :] = jnp.broadcast_to(y[None], (NALL, 1, HD))


def squares(yl, parts, cs):
    return pl.pallas_call(
        square_kernel,
        in_specs=[smem(), vmem(), vmem()],
        out_specs=vmem(),
        out_shape=jax.ShapeDtypeStruct((NALL, 2, HD), jnp.float32),
        compiler_params=pltpu.CompilerParams(vmem_limit_bytes=VMEM),
        cost_estimate=pl.CostEstimate(flops=10**6, bytes_accessed=10**6, transcendentals=0),
        name="square_sums",
    )(yl, parts, cs)


def swap(value, axis):
    return lax.ppermute(value, axis, [(0, 1), (1, 0)])


def body(queries, keys, values, out_grad, positions):
    kvi = (lax.axis_index("xh") * 4 + lax.axis_index("yh")).astype(jnp.int32).reshape(1)
    yl = lax.axis_index("yl").astype(jnp.int32)
    freq = jnp.asarray(frequencies())
    kv, cs = prep_keys(kvi, positions, freq, keys, values)
    kv_all = lax.all_to_all(kv, AX_Z, 0, 0)
    qg = prep_queries(positions, cs, queries, out_grad)
    other_x = swap(qg, AX_X)
    other_core = swap(qg, AX_C)
    other_both = swap(other_x, AX_C)
    qs, gs, qpos, order = sort_queries((qg, other_x, other_core, other_both))
    st, ks, s, d, perm = stats(order, qs, gs, qpos, kv_all)
    st_all = lax.all_to_all(st, QGROUP, 0, 0)
    dkv, keep, send = grads(perm, qs, gs, ks, s, d, st_all)
    near = swap(send, AX_C)
    far = swap(keep[2:] + near[2:], AX_X)
    parts = lax.all_to_all(dkv, KGROUP, 0, 0)
    sums = lax.all_to_all(squares(yl.reshape(1), parts, cs), ALLGROUP, 0, 0)
    sums = jnp.sum(sums, axis=0)
    query_grad = finish_dq(keep[:2], near[:2], far, cs)
    mine = lax.dynamic_slice_in_dim(sums, yl * (HD // 2), HD // 2, 1) / SEQ
    return query_grad, mine[0:1], mine[1:2]


def solution(mesh):
    inner = Mesh(
        mesh.devices.reshape(8, 2, 2, 2, 4, 2), (AX_Z, AX_X, AX_C, "xh", "yh", "yl")
    )
    ctx, head = (AX_Z, AX_X, AX_C), ("xh", "yh", "yl")
    return jax.shard_map(
        body,
        mesh=inner,
        in_specs=(P(ctx, head), P(ctx, None), P(ctx, None), P(ctx, head), P(ctx)),
        out_specs=(P(ctx, head), P(head, None), P(head, None)),
        check_vma=False,
    )
```
